32 devices in a mesh: fsdp: 8 (over z, x), ctx: 2 (over y), tp: 2 (over core).
Axes of the slice: x: 2, y: 2, z: 4, core: 2. Of those that a mesh axis runs over, the one named last changes fastest.
Arguments:
- tokens: bfloat16 [8, 2048, 768], P('fsdp', 'ctx'), may hold values from -6 to 6
- cotangent: float32 [8, 2048, 768], P('fsdp', 'ctx'), may hold values from -6 to 6
- lengths: int32 [8, 4], P('fsdp'), may hold values from 0 to 2048, as said below
- w_qkv: bfloat16 [3, 768, 768], P(None, 'fsdp', 'tp'), may hold values from -0.21875 to 0.21875
- w_out: bfloat16 [768, 768], P('tp', 'fsdp'), may hold values from -3.5 to 3.5
- w_up: bfloat16 [768, 3072], P('fsdp', 'tp'), may hold values from -0.21875 to 0.21875
- w_down: bfloat16 [3072, 768], P('tp', 'fsdp'), may hold values from -0.109375 to 0.109375
- qv_bias: float32 [2, 768], P(None, 'tp'), may hold values from -3 to 3
- up_bias: float32 [3072], P('tp'), may hold values from -3 to 3
- out_bias: float32 [2, 768], replicated, may hold values from -3 to 3
- gains: float32 [2, 768], replicated, may hold values from 0.25 to 1.75
- shifts: float32 [2, 768], replicated, may hold values from -3 to 3
Outputs:
- output: float32 [8, 2048, 768], P('fsdp', 'ctx')
- token_grad: float32 [8, 2048, 768], P('fsdp', 'ctx')
- qkv_grad: float32 [3, 768, 768], P(None, ('fsdp', 'ctx'), 'tp')
- out_proj_grad: float32 [768, 768], P('tp', ('fsdp', 'ctx'))
- up_grad: float32 [768, 3072], P(('fsdp', 'ctx'), 'tp')
- down_grad: float32 [3072, 768], P('tp', ('fsdp', 'ctx'))
- qv_bias_grad: float32 [2, 2, 384], P(None, 'tp', ('fsdp', 'ctx'))
- up_bias_grad: float32 [2, 1536], P('tp', ('fsdp', 'ctx'))
- out_bias_grad: float32 [2, 768], P(None, ('fsdp', 'ctx'))
- gains_grad: float32 [2, 768], P(None, ('fsdp', 'ctx'))
- shifts_grad: float32 [2, 768], P(None, ('fsdp', 'ctx'))
The draws below stay inside these ranges and needn't reach their ends.
Inputs may be any that keep to these rules, and one draw needn't show every extreme that they name: Each row holds 1 to 4 sequences in its first slots, each of 1024 positions or more, and zeros in the slots after them; the lengths of a row add up to 2048, its sequences follow one another from position 0 in the order given, and at least one row is a single sequence of 2048 positions.
All inputs are finite; a program needn't handle non-finite values.
Results may differ from the reference program's by a relative error of at most 0.015.
Values may be sent and summed in bfloat16 or wider, within the bound.
A program may use at most 192 MiB of HBM per device.

```python
import math
import jax
import jax.numpy as jnp
from jax import lax

D = 768
HEADS = 12
HD = 64
FF = 3072
NSEQ = 4
MIN_LEN = 1024
ROW_LEN = 2048
NROW = 8
N_TP = 2


def draw_lengths(key, part):
    key = jax.random.fold_in(key, 7)
    count_key, cut_key, pick_key = jax.random.split(key, 3)
    least = min(MIN_LEN, ROW_LEN)
    most_count = min(NSEQ, ROW_LEN // least)
    counts = jax.random.randint(count_key, (NROW,), 1, most_count + 1, dtype=jnp.int32)
    chosen = jax.random.randint(pick_key, (), 0, NROW, dtype=jnp.int32)
    counts = jnp.where(jnp.arange(NROW, dtype=jnp.int32) == chosen, 1, counts).astype(jnp.int32)
    extra = (ROW_LEN - counts * least).astype(jnp.int32)
    raw = jax.random.randint(cut_key, (NROW, NSEQ - 1), 0, 1 << 30, dtype=jnp.int32)
    raw = (raw % (extra[:, None] + 1)).astype(jnp.int32)
    ordered = jnp.sort(raw, axis=1)
    slot = jnp.arange(NSEQ - 1, dtype=jnp.int32)
    cuts = jnp.where(slot[None, :] < counts[:, None] - 1, ordered, extra[:, None]).astype(jnp.int32)
    edges = jnp.concatenate([jnp.zeros((NROW, 1), jnp.int32), cuts, extra[:, None]], axis=1)
    pieces = edges[:, 1:] - edges[:, :-1]
    active = (jnp.arange(NSEQ, dtype=jnp.int32)[None, :] < counts[:, None]).astype(jnp.int32)
    return (pieces + least * active).astype(jnp.int32)


def steps_of(own_key, extent, cuts, low, high):
    level = 1.0
    for dim, parts in cuts:
        heights = jax.random.uniform(jax.random.fold_in(jax.random.fold_in(own_key, 6), dim), (parts,), jnp.float32, low / len(cuts), high / len(cuts))
        level = level * jnp.repeat(jnp.exp(heights), extent[dim] // parts).reshape((-1,) + (1,) * (len(extent) - 1 - dim))
    return level


def centred(stream_key, shape, scale, most, cuts=(), held_as=jnp.bfloat16):
    drawn = scale * jax.random.normal(stream_key, shape, jnp.float32)
    if cuts:
        drawn = drawn * steps_of(stream_key, shape, cuts, -0.22, 0.18)
    return jnp.clip(drawn, -most, most).astype(held_as)


def setup_inputs(seed: int = 0) -> dict:
    arg_keys = jax.random.split(jax.random.key(seed), 13)
    tokens = centred(arg_keys[0], (NROW, ROW_LEN, D), 1.0, 6.0, ((0, 8), (1, 2)))
    cotangent = centred(arg_keys[1], (NROW, ROW_LEN, D), 1.0, 6.0, ((0, 8), (1, 2)), jnp.float32)
    lengths = draw_lengths(jax.random.fold_in(arg_keys[12], 71), 0)
    w_qkv = centred(arg_keys[3], (3, D, D), D ** -0.5, 0.21875, ((1, 8), (2, 2)))
    w_out = centred(arg_keys[4], (D, D), (D // 256) ** -0.5, 3.5, ((0, 2), (1, 8)))
    w_up = centred(arg_keys[5], (D, FF), D ** -0.5, 0.21875, ((0, 8), (1, 2)))
    w_down = centred(arg_keys[6], (FF, D), FF ** -0.5, 0.109375, ((0, 2), (1, 8)))
    qv_bias = centred(arg_keys[7], (2, D), 0.5, 3.0, ((1, 2),), jnp.float32)
    up_bias = centred(arg_keys[8], (FF,), 0.5, 3.0, ((0, 2),), jnp.float32)
    out_bias = centred(arg_keys[9], (2, D), 0.5, 3.0, (), jnp.float32)
    gains = jnp.clip(1.0 + 0.15 * jax.random.normal(arg_keys[10], (2, D), jnp.float32), 0.25, 1.75)
    shifts = centred(arg_keys[11], (2, D), 0.5, 3.0, (), jnp.float32)
    return {"tokens": tokens, "cotangent": cotangent, "lengths": lengths, "w_qkv": w_qkv, "w_out": w_out, "w_up": w_up, "w_down": w_down, "qv_bias": qv_bias, "up_bias": up_bias, "out_bias": out_bias, "gains": gains, "shifts": shifts}


EPSILON = 1e-05
HIGHEST_MODE = lax.Precision.HIGHEST

@jax.custom_vjp
def low(v):
    return lax.optimization_barrier(v.astype(jnp.bfloat16)).astype(jnp.float32)

@jax.custom_vjp
def low_back(v):
    return v

def low_keep(v):
    return (low(v), None)

def low_pass(kept, grad):
    return (grad,)

def back_keep(v):
    return (v, None)

def back_low(kept, grad):
    return (low(grad),)
low.defvjp(low_keep, low_pass)
low_back.defvjp(back_keep, back_low)

def normalize(values):
    centre = values - lax.optimization_barrier(jnp.mean(values, axis=-1, keepdims=True))
    variance = lax.optimization_barrier(jnp.mean(centre * centre, axis=-1, keepdims=True))
    return centre * lax.rsqrt(variance + EPSILON)

def matmul(left, right):
    return jnp.dot(left, right, precision=HIGHEST_MODE)

def attend(queries, keys, values, documents):
    block = math.gcd(ROW_LEN, 512)
    count = ROW_LEN // block
    positions = jnp.arange(ROW_LEN, dtype=jnp.int32)
    query_blocks = queries.reshape(count, block, HEADS, HD)
    pos_blocks = positions.reshape(count, block)
    doc_blocks = documents.reshape(count, block)
    key_heads = keys.reshape(ROW_LEN, HEADS, HD)
    value_heads = values.reshape(ROW_LEN, HEADS, HD)

    def one_block(inputs):
        query_part, query_pos, query_doc = inputs
        scores = jnp.einsum('qhd,khd->hqk', query_part, key_heads, precision=HIGHEST_MODE) * HD ** (-0.5)
        scores = low_back(scores)
        allowed = (positions[None, :] <= query_pos[:, None]) & (documents[None, :] == query_doc[:, None])
        scores = jnp.where(allowed[None], scores, -1e+30)
        weights = low(jax.nn.softmax(scores, axis=-1))
        return jnp.einsum('hqk,khd->qhd', weights, value_heads, precision=HIGHEST_MODE)
    outputs = lax.map(jax.checkpoint(one_block), (query_blocks, pos_blocks, doc_blocks))
    return outputs.reshape(ROW_LEN, D)

def layer_row(stream, documents, params):
    w_qkv, w_out, w_up, w_down, qv_bias, up_bias, out_bias, gains, shifts = params
    normed = normalize(stream)
    hidden = low(normed * gains[0] + shifts[0])
    queries = low(low_back(matmul(hidden, w_qkv[0]) + qv_bias[0]))
    keys = low(low_back(matmul(hidden, w_qkv[1])))
    values = low(low_back(matmul(hidden, w_qkv[2]) + qv_bias[1]))
    mixed = low(low_back(attend(queries, keys, values, documents)))
    branch = low_back(matmul(mixed, w_out) + out_bias[0])
    middle = stream + branch
    hidden_two = low(normalize(middle) * gains[1] + shifts[1])
    pre_act = low_back(matmul(hidden_two, w_up) + up_bias)
    activ = low(jax.nn.gelu(pre_act, approximate=True))
    branch_two = low_back(matmul(activ, w_down) + out_bias[1])
    return middle + branch_two

def forward(stream, documents, params):

    def row_step(state, inputs):
        return (state, layer_row(inputs[0], inputs[1], params))
    _, outputs = lax.scan(row_step, jnp.zeros((), jnp.float32), (stream, documents))
    return outputs

def reference(tokens, cotangent, lengths, w_qkv, w_out, w_up, w_down, qv_bias, up_bias, out_bias, gains, shifts):
    starts = (jnp.cumsum(lengths, axis=1, dtype=jnp.int32) - lengths).astype(jnp.int32)
    positions = jnp.arange(ROW_LEN, dtype=jnp.int32)
    documents = (lax.optimization_barrier(jnp.sum((positions[None, :, None] >= starts[:, None, :]).astype(jnp.int32), axis=2)) - 1).astype(jnp.int32)
    floats = [array.astype(jnp.float32) for array in (tokens, w_qkv, w_out, w_up, w_down, qv_bias, up_bias, out_bias, gains, shifts)]

    def whole(stream, *params):
        return forward(stream, documents, params)
    output, pullback = jax.vjp(whole, *floats)
    grads = pullback(cotangent.astype(jnp.float32))
    token_grad, qkv_grad, out_proj_grad, up_grad, down_grad, qv_grad, up_bias_grad, out_bias_grad, gains_grad, shifts_grad = grads
    return (output, token_grad, qkv_grad, out_proj_grad, up_grad, down_grad, qv_grad.reshape(2, N_TP, D // N_TP), up_bias_grad.reshape(N_TP, FF // N_TP), out_bias_grad, gains_grad, shifts_grad)
```

```python
import math

import jax
import jax.numpy as jnp
from jax import lax
from jax.sharding import PartitionSpec as P

HD = 64


EPSILON = 1e-05
NEG_LARGE = -1e30


def normalize(values):
    centre = values - jnp.mean(values, axis=-1, keepdims=True)
    variance = jnp.mean(centre * centre, axis=-1, keepdims=True)
    inv_std = lax.rsqrt(variance + EPSILON)
    return (centre * inv_std, inv_std)


def norm_back(grad_in, normed, inv_std):
    mean_grad = jnp.mean(grad_in, axis=-1, keepdims=True)
    mean_cross = jnp.mean(grad_in * normed, axis=-1, keepdims=True)
    return inv_std * (grad_in - mean_grad - normed * mean_cross)


def gelu_curve(values):
    return jax.nn.gelu(values, approximate=True)


def bits_of(axis):
    size = lax.axis_size(axis)
    return [(axis, bit) for bit in range(size.bit_length() - 1)]


def swap(values, axis, bit):
    size = lax.axis_size(axis)
    return lax.ppermute(values, axis, [(i, i ^ (1 << bit)) for i in range(size)])


def gather_rows(shard, axis):
    size = lax.axis_size(axis)
    here = lax.axis_index(axis)
    rows = shard.shape[0]
    held = shard
    offsets = [0]
    for _, bit in reversed(bits_of(axis)):
        held = jnp.concatenate([held, swap(held, axis, bit)], axis=0)
        offsets = offsets + [offset ^ (1 << bit) for offset in offsets]
    place = [offsets.index(offset) for offset in range(size)]
    place = jnp.array(place, jnp.int32)
    parts = [
        lax.dynamic_slice_in_dim(held, place[jnp.bitwise_xor(here, i)] * rows, rows, 0)
        for i in range(size)
    ]
    return jnp.concatenate(parts, axis=0)


def scatter_rows(terms, order):
    fsdp_bits, ctx_bits = len(bits_of("fsdp")), len(bits_of("ctx"))
    count = fsdp_bits + ctx_bits
    held = terms.reshape((2,) * count + (terms.shape[0] >> count,) + terms.shape[1:])
    for step, (axis, bit) in enumerate(order):
        dim = fsdp_bits - 1 - bit if axis == "fsdp" else count - 1 - bit
        mine = (lax.axis_index(axis) >> bit) & 1
        send = lax.dynamic_index_in_dim(held, 1 - mine, dim, keepdims=True)
        keep = lax.dynamic_index_in_dim(held, mine, dim, keepdims=True)
        held = keep.astype(jnp.float32) + swap(send, axis, bit).astype(jnp.float32)
        if step < count - 1:
            held = held.astype(terms.dtype)
    return held.reshape(held.shape[count:])


def pair_sum(partial):
    sent = partial.astype(jnp.bfloat16)
    total = sent.astype(jnp.float32)
    for axis, bit in bits_of("tp"):
        total = total + swap(total.astype(jnp.bfloat16), axis, bit).astype(jnp.float32)
    return total


def per_device(
    tokens,
    cotangent,
    lengths,
    w_qkv,
    w_out,
    w_up,
    w_down,
    qv_bias,
    up_bias,
    out_bias,
    gains,
    shifts,
):
    stream = tokens[0].astype(jnp.float32)
    grad_out = cotangent[0]
    seg_len = stream.shape[0]
    ctx_count = lax.axis_size("ctx")
    ctx_here = lax.axis_index("ctx")
    row_len = seg_len * ctx_count
    first_pos = ctx_here * seg_len
    seq_lens = lengths[0]
    seq_starts = jnp.cumsum(seq_lens, dtype=jnp.int32) - seq_lens

    def doc_of(spots):
        return jnp.sum((spots[:, None] >= seq_starts[None, :]).astype(jnp.int32), axis=1) - 1

    query_pos = first_pos + jnp.arange(seg_len, dtype=jnp.int32)
    query_doc = doc_of(query_pos)
    all_pos = jnp.arange(row_len, dtype=jnp.int32)
    all_doc = doc_of(all_pos)
    local_width = w_qkv.shape[2]
    heads_dev = local_width // HD
    block = math.gcd(row_len, 512)
    block_count = row_len // block
    scale = HD ** (-0.5)
    block_last_doc = all_doc.reshape(block_count, block)[:, block - 1]
    first_block = jnp.sum((block_last_doc < query_doc[0]).astype(jnp.int32))
    end_block = (first_pos + seg_len - 1) // block + 1
    qkv_rows = gather_rows(w_qkv.transpose(1, 0, 2), "fsdp")
    out_rows = gather_rows(w_out.T, "fsdp")
    up_full = gather_rows(w_up, "fsdp")
    down_rows = gather_rows(w_down.T, "fsdp")
    normed, inv_std = normalize(stream)
    hidden = (normed * gains[0] + shifts[0]).astype(jnp.bfloat16)
    projected = jnp.einsum("td,dce->cte", hidden, qkv_rows, preferred_element_type=jnp.float32)
    queries = (projected[0] + qv_bias[0]).astype(jnp.bfloat16)
    keys_local = projected[1].astype(jnp.bfloat16)
    values_local = (projected[2] + qv_bias[1]).astype(jnp.bfloat16)
    all_pairs = gather_rows(jnp.concatenate([keys_local, values_local], axis=1), "ctx")
    all_keys, all_values = all_pairs[:, :local_width], all_pairs[:, local_width:]
    query_heads = queries.reshape(seg_len, heads_dev, HD)

    def take_block(source, block_id):
        return lax.dynamic_slice_in_dim(source, block_id * block, block, 0).reshape(
            block, heads_dev, HD
        )

    def block_scores(key_part, block_id):
        key_pos = lax.dynamic_slice_in_dim(all_pos, block_id * block, block, 0)
        key_doc = lax.dynamic_slice_in_dim(all_doc, block_id * block, block, 0)
        scores = (
            jnp.einsum("qhd,khd->hqk", query_heads, key_part, preferred_element_type=jnp.float32)
            * scale
        )
        allowed = (key_pos[None, :] <= query_pos[:, None]) & (
            key_doc[None, :] == query_doc[:, None]
        )
        return (scores, allowed[None])

    def max_step(block_id, running):
        run_max, run_sum = running
        scores, allowed = block_scores(take_block(all_keys, block_id), block_id)
        masked = jnp.where(allowed, scores, NEG_LARGE)
        new_max = jnp.maximum(run_max, jnp.max(masked, axis=-1))
        weights = jnp.where(allowed, jnp.exp(masked - new_max[..., None]), 0.0)
        return (new_max, run_sum * jnp.exp(run_max - new_max) + jnp.sum(weights, axis=-1))

    start_state = (
        jnp.full((heads_dev, seg_len), NEG_LARGE, jnp.float32),
        jnp.zeros((heads_dev, seg_len), jnp.float32),
    )
    run_max, run_sum = lax.fori_loop(first_block, end_block, max_step, start_state)
    log_total = run_max + jnp.log(run_sum)

    def probs_of(scores, allowed):
        return jnp.where(
            allowed, jnp.exp(jnp.where(allowed, scores, NEG_LARGE) - log_total[..., None]), 0.0
        )

    def mix_step(block_id, totals):
        scores, allowed = block_scores(take_block(all_keys, block_id), block_id)
        weights = probs_of(scores, allowed).astype(jnp.bfloat16)
        value_part = take_block(all_values, block_id)
        return totals + jnp.einsum(
            "hqk,khd->hqd", weights, value_part, preferred_element_type=jnp.float32
        )

    mixed_total = lax.fori_loop(
        first_block, end_block, mix_step, jnp.zeros((heads_dev, seg_len, HD), jnp.float32)
    )
    mixed = mixed_total.transpose(1, 0, 2).reshape(seg_len, local_width).astype(jnp.bfloat16)
    partial_attn = jnp.einsum("tc,ec->te", mixed, out_rows, preferred_element_type=jnp.float32)
    middle = (
        stream + pair_sum(partial_attn) + out_bias[0]
    )
    normed_two, inv_two = normalize(middle)
    hidden_two = (normed_two * gains[1] + shifts[1]).astype(jnp.bfloat16)
    pre_act = jnp.dot(hidden_two, up_full, preferred_element_type=jnp.float32) + up_bias
    activ_exact, gelu_pull = jax.vjp(gelu_curve, pre_act)
    activ = activ_exact.astype(jnp.bfloat16)
    partial_ff = jnp.einsum("tf,ef->te", activ, down_rows, preferred_element_type=jnp.float32)
    output = (
        middle + pair_sum(partial_ff) + out_bias[1]
    )
    down_in = grad_out.astype(jnp.bfloat16)
    act_grad = jnp.einsum("te,ef->tf", down_in, down_rows, preferred_element_type=jnp.float32)
    pre_grad = gelu_pull(act_grad)[0].astype(jnp.bfloat16)
    partial_two = jnp.einsum("tf,df->td", pre_grad, up_full, preferred_element_type=jnp.float32)
    hidden_two_grad = pair_sum(partial_two)
    middle_grad = grad_out + norm_back(hidden_two_grad * gains[1], normed_two, inv_two)
    attn_in = middle_grad.astype(jnp.bfloat16)
    mixed_grad = jnp.einsum(
        "te,ec->tc", attn_in, out_rows, preferred_element_type=jnp.float32
    ).astype(jnp.bfloat16)
    grad_heads = mixed_grad.reshape(seg_len, heads_dev, HD)
    delta = jnp.einsum("qhd,hqd->hq", grad_heads.astype(jnp.float32), mixed_total)

    def grad_step(block_id, carry):
        query_total, key_buffer, value_buffer = carry
        key_part = take_block(all_keys, block_id)
        value_part = take_block(all_values, block_id)
        scores, allowed = block_scores(key_part, block_id)
        weights = probs_of(scores, allowed)
        weight_grad = jnp.einsum(
            "qhd,khd->hqk", grad_heads, value_part, preferred_element_type=jnp.float32
        )
        score_grad = (weights * (weight_grad - delta[..., None])).astype(jnp.bfloat16)
        query_total = query_total + jnp.einsum(
            "hqk,khd->hqd", score_grad, key_part, preferred_element_type=jnp.float32
        )
        key_term = (
            jnp.einsum("hqk,qhd->khd", score_grad, query_heads, preferred_element_type=jnp.float32)
            * scale
        )
        value_term = jnp.einsum(
            "hqk,qhd->khd",
            weights.astype(jnp.bfloat16),
            grad_heads,
            preferred_element_type=jnp.float32,
        )
        key_buffer = lax.dynamic_update_slice_in_dim(
            key_buffer, key_term.reshape(block, local_width), block_id * block, 0
        )
        value_buffer = lax.dynamic_update_slice_in_dim(
            value_buffer, value_term.reshape(block, local_width), block_id * block, 0
        )
        return (query_total, key_buffer, value_buffer)

    empty_row = jnp.zeros((row_len, local_width), jnp.float32)
    query_total, key_terms, value_terms = lax.fori_loop(
        first_block,
        end_block,
        grad_step,
        (jnp.zeros((heads_dev, seg_len, HD), jnp.float32), empty_row, empty_row),
    )
    pair_terms = jnp.concatenate([key_terms, value_terms], axis=1).astype(jnp.bfloat16)
    pair_grad = pair_terms.reshape(ctx_count, seg_len, 2 * local_width)
    for axis, bit in reversed(bits_of("ctx")):
        split = pair_grad.reshape((2, pair_grad.shape[0] // 2) + pair_grad.shape[1:])
        mine = (ctx_here >> bit) & 1
        send = lax.dynamic_index_in_dim(split, 1 - mine, 0, keepdims=False)
        keep = lax.dynamic_index_in_dim(split, mine, 0, keepdims=False)
        pair_grad = keep.astype(jnp.float32) + swap(send, axis, bit).astype(jnp.float32)
        pair_grad = pair_grad.astype(jnp.bfloat16)
    key_grad, value_grad = pair_grad[0][:, :local_width], pair_grad[0][:, local_width:]
    query_grad = query_total.transpose(1, 0, 2).reshape(seg_len, local_width) * scale
    qkv_grad_in = jnp.stack([query_grad.astype(jnp.bfloat16), key_grad, value_grad], axis=1)
    partial_hidden = jnp.einsum(
        "tce,dce->td", qkv_grad_in, qkv_rows, preferred_element_type=jnp.float32
    )
    hidden_grad = pair_sum(partial_hidden)
    token_grad = middle_grad + norm_back(hidden_grad * gains[0], normed, inv_std)
    qkv_term = jnp.einsum("td,tce->dce", hidden, qkv_grad_in, preferred_element_type=jnp.float32)
    out_term = jnp.einsum("te,tc->ec", attn_in, mixed, preferred_element_type=jnp.float32)
    up_term = jnp.einsum("td,tf->df", hidden_two, pre_grad, preferred_element_type=jnp.float32)
    down_term = jnp.einsum("te,tf->ef", down_in, activ, preferred_element_type=jnp.float32)
    qv_term = jnp.stack(
        [
            jnp.sum(qkv_grad_in[:, 0].astype(jnp.float32), axis=0),
            jnp.sum(qkv_grad_in[:, 2].astype(jnp.float32), axis=0),
        ]
    )
    up_bias_term = jnp.sum(pre_grad.astype(jnp.float32), axis=0)
    out_bias_term = jnp.stack(
        [jnp.sum(attn_in.astype(jnp.float32), axis=0), jnp.sum(down_in.astype(jnp.float32), axis=0)]
    )
    gains_term = jnp.stack(
        [jnp.sum(hidden_grad * normed, axis=0), jnp.sum(hidden_two_grad * normed_two, axis=0)]
    )
    shifts_term = jnp.stack([jnp.sum(hidden_grad, axis=0), jnp.sum(hidden_two_grad, axis=0)])
    along_ctx, along_fsdp = bits_of("ctx"), bits_of("fsdp")
    ctx_first = along_ctx + along_fsdp
    fsdp_first = along_fsdp[:1] + along_ctx + along_fsdp[1:]
    parts = lax.axis_size("fsdp") * ctx_count
    down_sum = scatter_rows(down_term.astype(jnp.bfloat16), ctx_first)
    up_sum = scatter_rows(up_term.astype(jnp.bfloat16), fsdp_first)
    out_sum = scatter_rows(out_term.astype(jnp.bfloat16), ctx_first)
    qkv_sum = scatter_rows(
        qkv_term.astype(jnp.bfloat16).reshape(qkv_term.shape[0], 3 * local_width), ctx_first
    )

    def in_parts(term):
        lead = term.shape[0]
        return term.reshape(lead, parts, -1).transpose(1, 0, 2).reshape(parts, -1)

    small = [qv_term, up_bias_term[None], out_bias_term, gains_term, shifts_term]
    small_sum = scatter_rows(
        jnp.concatenate([in_parts(term) for term in small], axis=1), ctx_first
    ).reshape(-1)
    small_sums = []
    start = 0
    for term in small:
        size = term.size // parts
        small_sums.append(small_sum[start : start + size].reshape(term.shape[0], -1))
        start += size
    return (
        output[None],
        token_grad[None],
        qkv_sum.reshape(-1, 3, local_width).transpose(1, 0, 2),
        out_sum.T,
        up_sum,
        down_sum.T,
        small_sums[0][:, None, :],
        small_sums[1],
        small_sums[2],
        small_sums[3],
        small_sums[4],
    )


def solution(mesh):
    placed = (
        P("fsdp", "ctx", None),
        P("fsdp", "ctx", None),
        P("fsdp", None),
        P(None, "fsdp", "tp"),
        P("tp", "fsdp"),
        P("fsdp", "tp"),
        P("tp", "fsdp"),
        P(None, "tp"),
        P("tp"),
        P(),
        P(),
        P(),
    )
    return jax.shard_map(
        per_device,
        mesh=mesh,
        in_specs=placed,
        out_specs=(
            P("fsdp", "ctx", None),
            P("fsdp", "ctx", None),
            P(None, ("fsdp", "ctx"), "tp"),
            P("tp", ("fsdp", "ctx")),
            P(("fsdp", "ctx"), "tp"),
            P("tp", ("fsdp", "ctx")),
            P(None, "tp", ("fsdp", "ctx")),
            P("tp", ("fsdp", "ctx")),
            P(None, ("fsdp", "ctx")),
            P(None, ("fsdp", "ctx")),
            P(None, ("fsdp", "ctx")),
        ),
        check_vma=False,
    )
```

```python
import functools

import jax
import jax.numpy as jnp
from jax import lax
from jax.experimental import pallas as pl
from jax.experimental.pallas import tpu as pltpu
from jax.sharding import PartitionSpec as P

HD = 64


EPSILON = 1e-05
NEG_LARGE = -1e30


def normalize(values):
    centre = values - jnp.mean(values, axis=-1, keepdims=True)
    variance = jnp.mean(centre * centre, axis=-1, keepdims=True)
    inv_std = lax.rsqrt(variance + EPSILON)
    return (centre * inv_std, inv_std)


def norm_back(grad_in, normed, inv_std):
    mean_grad = jnp.mean(grad_in, axis=-1, keepdims=True)
    mean_cross = jnp.mean(grad_in * normed, axis=-1, keepdims=True)
    return inv_std * (grad_in - mean_grad - normed * mean_cross)


def gelu_curve(values):
    return jax.nn.gelu(values, approximate=True)


def bits_of(axis):
    size = lax.axis_size(axis)
    return [(axis, bit) for bit in range(size.bit_length() - 1)]


def swap(values, axis, bit):
    size = lax.axis_size(axis)
    return lax.ppermute(values, axis, [(i, i ^ (1 << bit)) for i in range(size)])


def gather_rows(shard, axis):
    size = lax.axis_size(axis)
    here = lax.axis_index(axis)
    rows = shard.shape[0]
    held = shard
    offsets = [0]
    for _, bit in reversed(bits_of(axis)):
        held = jnp.concatenate([held, swap(held, axis, bit)], axis=0)
        offsets = offsets + [offset ^ (1 << bit) for offset in offsets]
    place = [offsets.index(offset) for offset in range(size)]
    place = jnp.array(place, jnp.int32)
    parts = [
        lax.dynamic_slice_in_dim(held, place[jnp.bitwise_xor(here, i)] * rows, rows, 0)
        for i in range(size)
    ]
    return jnp.concatenate(parts, axis=0)


def scatter_rows(terms, order):
    fsdp_bits, ctx_bits = len(bits_of("fsdp")), len(bits_of("ctx"))
    count = fsdp_bits + ctx_bits
    held = terms.reshape((2,) * count + (terms.shape[0] >> count,) + terms.shape[1:])
    for step, (axis, bit) in enumerate(order):
        dim = fsdp_bits - 1 - bit if axis == "fsdp" else count - 1 - bit
        mine = (lax.axis_index(axis) >> bit) & 1
        send = lax.dynamic_index_in_dim(held, 1 - mine, dim, keepdims=True)
        keep = lax.dynamic_index_in_dim(held, mine, dim, keepdims=True)
        held = keep.astype(jnp.float32) + swap(send, axis, bit).astype(jnp.float32)
        if step < count - 1:
            held = held.astype(terms.dtype)
    return held.reshape(held.shape[count:])


def pair_sum(partial):
    sent = partial.astype(jnp.bfloat16)
    total = sent.astype(jnp.float32)
    for axis, bit in bits_of("tp"):
        total = total + swap(total.astype(jnp.bfloat16), axis, bit).astype(jnp.float32)
    return total


BLOCK_Q = 512
BLOCK_K = 512
PAIR = 2 * HD


def half_mask(shape, dim, half):
    spots = lax.broadcasted_iota(jnp.int32, shape, dim)
    inside = (spots >= half * HD) & (spots < (half + 1) * HD)
    return jnp.where(inside, 1.0, 0.0).astype(jnp.bfloat16)


def allowed_pairs(shape, key_start, query_start, begin):
    key_pos = key_start + lax.broadcasted_iota(jnp.int32, shape, 0)
    query_pos = query_start + lax.broadcasted_iota(jnp.int32, shape, 1)
    return (key_pos <= query_pos) & (key_pos >= begin)


def mix_kernel(bounds, q_ref, k_ref, v_ref, begin_ref, mix_ref, total_ref, lse_ref, vt_ref):
    step = pl.program_id(1)
    width = q_ref.shape[0]
    block = min(BLOCK_K, k_ref.shape[0])

    @pl.when(step == 0)
    def _():
        vt_ref[...] = v_ref[...].T

    query_t = (q_ref[...] * jnp.bfloat16(0.125)).T
    query_parts = [query_t * half_mask(query_t.shape, 0, half) for half in range(2)]
    begin = begin_ref[...]
    query_start = bounds[4, step]

    def body(masked, block_id, carry):
        start = pl.multiple_of(block_id * block, block)
        keys = k_ref[pl.ds(start, block), :]
        if masked:
            allowed = allowed_pairs((block, width), start, query_start, begin)
        out = []
        for half in range(2):
            run_max, run_sum, total = carry[half]
            scores = jnp.dot(keys, query_parts[half], preferred_element_type=jnp.float32)
            if masked:
                scores = jnp.where(allowed, scores, NEG_LARGE)
            new_max = jnp.maximum(run_max, jnp.max(scores, axis=0, keepdims=True))
            weights = jnp.exp(scores - new_max)
            decay = jnp.exp(run_max - new_max)
            values_t = vt_ref[half * HD : (half + 1) * HD, pl.ds(start, block)]
            out.append(
                (
                    new_max,
                    run_sum * decay + jnp.sum(weights, axis=0, keepdims=True),
                    total * decay
                    + jnp.dot(
                        values_t, weights.astype(jnp.bfloat16), preferred_element_type=jnp.float32
                    ),
                )
            )
        return tuple(out)

    empty = (
        jnp.full((1, width), NEG_LARGE, jnp.float32),
        jnp.zeros((1, width), jnp.float32),
        jnp.zeros((HD, width), jnp.float32),
    )
    carry = (empty, empty)
    for part, masked in enumerate((True, False, True)):
        carry = lax.fori_loop(
            bounds[part, step], bounds[part + 1, step], functools.partial(body, masked), carry
        )
    for half in range(2):
        run_max, run_sum, total = carry[half]
        total_ref[half * HD : (half + 1) * HD, :] = total / run_sum
        lse_ref[0, half : half + 1, :] = run_max + jnp.log(run_sum)
    mix_ref[...] = total_ref[...].T.astype(jnp.bfloat16)


def grad_kernel(
    bounds, q_ref, g_ref, k_ref, v_ref, begin_ref, total_ref, lse_ref,
    dq_ref, dkv_ref, kt_ref, dk_ref, dv_ref,
):
    step = pl.program_id(1)
    width = q_ref.shape[0]
    block = min(BLOCK_K, k_ref.shape[0])

    @pl.when(step == 0)
    def _():
        kt_ref[...] = k_ref[...].T
        dk_ref[...] = jnp.zeros_like(dk_ref)
        dv_ref[...] = jnp.zeros_like(dv_ref)

    query = q_ref[...] * jnp.bfloat16(0.125)
    grad = g_ref[...]
    query_t = query.T
    grad_t = grad.T
    product = grad_t.astype(jnp.float32) * total_ref[...]
    parts = []
    for half in range(2):
        down = half_mask(query_t.shape, 0, half)
        along = half_mask(query.shape, 1, half)
        parts.append(
            (
                query * along,
                query_t * down,
                grad * along,
                grad_t * down,
                jnp.sum(product[half * HD : (half + 1) * HD, :], axis=0, keepdims=True),
                lse_ref[0, half : half + 1, :],
            )
        )
    begin = begin_ref[...]
    query_start = bounds[4, step]

    def body(masked, block_id, carry):
        start = pl.multiple_of(block_id * block, block)
        spots = pl.ds(start, block)
        keys = k_ref[spots, :]
        values = v_ref[spots, :]
        if masked:
            allowed = allowed_pairs((block, width), start, query_start, begin)
        out = []
        key_sum = dk_ref[spots, :]
        value_sum = dv_ref[spots, :]
        for half in range(2):
            query_n, query_t, grad_n, grad_t, delta, lse = parts[half]
            scores = jnp.dot(keys, query_t, preferred_element_type=jnp.float32)
            if masked:
                scores = jnp.where(allowed, scores, NEG_LARGE)
            weights = jnp.exp(scores - lse)
            weight_grad = jnp.dot(values, grad_t, preferred_element_type=jnp.float32)
            score_grad = (weights * (weight_grad - delta)).astype(jnp.bfloat16)
            value_sum = value_sum + jnp.dot(
                weights.astype(jnp.bfloat16), grad_n, preferred_element_type=jnp.float32
            )
            key_sum = key_sum + jnp.dot(score_grad, query_n, preferred_element_type=jnp.float32)
            keys_t = kt_ref[half * HD : (half + 1) * HD, spots]
            out.append(
                carry[half] + jnp.dot(keys_t, score_grad, preferred_element_type=jnp.float32)
            )
        dk_ref[spots, :] = key_sum
        dv_ref[spots, :] = value_sum
        return tuple(out)

    carry = (jnp.zeros((HD, width), jnp.float32),) * 2
    for part, masked in enumerate((True, False, True)):
        carry = lax.fori_loop(
            bounds[part, step], bounds[part + 1, step], functools.partial(body, masked), carry
        )
    dq_ref[...] = (jnp.concatenate(carry, axis=0) * 0.125).T.astype(jnp.bfloat16)

    @pl.when(step == pl.num_programs(1) - 1)
    def _():
        dkv_ref[0] = dk_ref[...].astype(jnp.bfloat16)
        dkv_ref[1] = dv_ref[...].astype(jnp.bfloat16)


def attention_bounds(first_pos, seg_len, row_len, begins):
    width, block = min(BLOCK_Q, seg_len), min(BLOCK_K, row_len)
    count = seg_len // width
    starts = first_pos + jnp.arange(count, dtype=jnp.int32) * width
    low = begins[::width] // block
    end = (starts + width - 1) // block + 1
    inner = jnp.clip((begins[width - 1 :: width] + block - 1) // block, low, end)
    outer = jnp.clip((starts + 1) // block, inner, end)
    return jnp.stack([low, inner, outer, end, starts]).astype(jnp.int32)


def attend(bounds, begins, queries, pairs):
    seg_len, local_width = queries.shape
    row_len = pairs.shape[0]
    count = local_width // PAIR
    width = min(BLOCK_Q, seg_len)
    work = count * 2 * seg_len * row_len
    return pl.pallas_call(
        mix_kernel,
        grid_spec=pltpu.PrefetchScalarGridSpec(
            num_scalar_prefetch=1,
            grid=(count, seg_len // width),
            in_specs=[
                pl.BlockSpec((width, PAIR), lambda p, i, b: (i, p)),
                pl.BlockSpec((row_len, PAIR), lambda p, i, b: (0, p)),
                pl.BlockSpec((row_len, PAIR), lambda p, i, b: (0, p + count)),
                pl.BlockSpec((1, width), lambda p, i, b: (0, i)),
            ],
            out_specs=[
                pl.BlockSpec((width, PAIR), lambda p, i, b: (i, p)),
                pl.BlockSpec((PAIR, width), lambda p, i, b: (p, i)),
                pl.BlockSpec((1, 2, width), lambda p, i, b: (p, 0, i)),
            ],
            scratch_shapes=[pltpu.VMEM((PAIR, row_len), jnp.bfloat16)],
        ),
        out_shape=[
            jax.ShapeDtypeStruct((seg_len, local_width), jnp.bfloat16),
            jax.ShapeDtypeStruct((local_width, seg_len), jnp.float32),
            jax.ShapeDtypeStruct((count, 2, seg_len), jnp.float32),
        ],
        compiler_params=pltpu.CompilerParams(vmem_limit_bytes=48 * 1024 * 1024),
        cost_estimate=pl.CostEstimate(
            flops=work * 4 * PAIR, bytes_accessed=6 * 2**20, transcendentals=work
        ),
        name="attn_mix",
    )(bounds, queries, pairs, pairs, begins[None])


def attend_back(bounds, begins, queries, grads, pairs, totals, lse):
    seg_len, local_width = queries.shape
    row_len = pairs.shape[0]
    count = local_width // PAIR
    width = min(BLOCK_Q, seg_len)
    work = count * 2 * seg_len * row_len
    return pl.pallas_call(
        grad_kernel,
        grid_spec=pltpu.PrefetchScalarGridSpec(
            num_scalar_prefetch=1,
            grid=(count, seg_len // width),
            in_specs=[
                pl.BlockSpec((width, PAIR), lambda p, i, b: (i, p)),
                pl.BlockSpec((width, PAIR), lambda p, i, b: (i, p)),
                pl.BlockSpec((row_len, PAIR), lambda p, i, b: (0, p)),
                pl.BlockSpec((row_len, PAIR), lambda p, i, b: (0, p + count)),
                pl.BlockSpec((1, width), lambda p, i, b: (0, i)),
                pl.BlockSpec((PAIR, width), lambda p, i, b: (p, i)),
                pl.BlockSpec((1, 2, width), lambda p, i, b: (p, 0, i)),
            ],
            out_specs=[
                pl.BlockSpec((width, PAIR), lambda p, i, b: (i, p)),
                pl.BlockSpec((2, row_len, PAIR), lambda p, i, b: (0, 0, p)),
            ],
            scratch_shapes=[
                pltpu.VMEM((PAIR, row_len), jnp.bfloat16),
                pltpu.VMEM((row_len, PAIR), jnp.float32),
                pltpu.VMEM((row_len, PAIR), jnp.float32),
            ],
        ),
        out_shape=[
            jax.ShapeDtypeStruct((seg_len, local_width), jnp.bfloat16),
            jax.ShapeDtypeStruct((2, row_len, local_width), jnp.bfloat16),
        ],
        compiler_params=pltpu.CompilerParams(vmem_limit_bytes=48 * 1024 * 1024),
        cost_estimate=pl.CostEstimate(
            flops=work * 8 * PAIR, bytes_accessed=12 * 2**20, transcendentals=work
        ),
        name="attn_grad",
    )(bounds, queries, grads, pairs, pairs, begins[None], totals, lse)


def per_device(
    tokens,
    cotangent,
    lengths,
    w_qkv,
    w_out,
    w_up,
    w_down,
    qv_bias,
    up_bias,
    out_bias,
    gains,
    shifts,
):
    stream = tokens[0].astype(jnp.float32)
    grad_out = cotangent[0]
    seg_len = stream.shape[0]
    ctx_count = lax.axis_size("ctx")
    ctx_here = lax.axis_index("ctx")
    row_len = seg_len * ctx_count
    first_pos = ctx_here * seg_len
    seq_lens = lengths[0]
    seq_starts = jnp.cumsum(seq_lens, dtype=jnp.int32) - seq_lens

    query_pos = first_pos + jnp.arange(seg_len, dtype=jnp.int32)
    begins = jnp.max(
        jnp.where(query_pos[:, None] >= seq_starts[None, :], seq_starts[None, :], 0), axis=1
    ).astype(jnp.int32)
    local_width = w_qkv.shape[2]
    bounds = attention_bounds(first_pos, seg_len, row_len, begins)
    qkv_rows = gather_rows(jnp.concatenate([w_qkv[0], w_qkv[1], w_qkv[2]], axis=1), "fsdp")
    qkv_rows, w_out, w_up, w_down = lax.optimization_barrier((qkv_rows, w_out, w_up, w_down))
    both_rows = gather_rows(jnp.concatenate([w_up, w_out.T], axis=1), "fsdp")
    up_full, out_rows = both_rows[:, : w_up.shape[1]], both_rows[:, w_up.shape[1] :]
    down_rows = gather_rows(w_down.T, "fsdp")
    normed, inv_std = normalize(stream)
    hidden = (normed * gains[0] + shifts[0]).astype(jnp.bfloat16)
    projected = jnp.dot(hidden, qkv_rows, preferred_element_type=jnp.float32)
    queries = (projected[:, :local_width] + qv_bias[0]).astype(jnp.bfloat16)
    pair_bias = jnp.concatenate([jnp.zeros_like(qv_bias[1]), qv_bias[1]])
    pairs = (projected[:, local_width:] + pair_bias).astype(jnp.bfloat16)
    all_pairs = gather_rows(pairs, "ctx")
    mixed, mixed_total, log_total = attend(bounds, begins, queries, all_pairs)
    partial_attn = jnp.einsum("tc,ec->te", mixed, out_rows, preferred_element_type=jnp.float32)
    middle = (
        stream + pair_sum(partial_attn) + out_bias[0]
    )
    normed_two, inv_two = normalize(middle)
    hidden_two = (normed_two * gains[1] + shifts[1]).astype(jnp.bfloat16)
    pre_act = jnp.dot(hidden_two, up_full, preferred_element_type=jnp.float32) + up_bias
    activ_exact, gelu_pull = jax.vjp(gelu_curve, pre_act)
    activ = activ_exact.astype(jnp.bfloat16)
    partial_ff = jnp.einsum("tf,ef->te", activ, down_rows, preferred_element_type=jnp.float32)
    output = (
        middle + pair_sum(partial_ff) + out_bias[1]
    )
    down_in = grad_out.astype(jnp.bfloat16)
    act_grad = jnp.einsum("te,ef->tf", down_in, down_rows, preferred_element_type=jnp.float32)
    pre_grad = gelu_pull(act_grad)[0].astype(jnp.bfloat16)
    partial_two = jnp.einsum("tf,df->td", pre_grad, up_full, preferred_element_type=jnp.float32)
    hidden_two_grad = pair_sum(partial_two)
    middle_grad = grad_out + norm_back(hidden_two_grad * gains[1], normed_two, inv_two)
    attn_in = middle_grad.astype(jnp.bfloat16)
    mixed_grad = jnp.einsum(
        "te,ec->tc", attn_in, out_rows, preferred_element_type=jnp.float32
    ).astype(jnp.bfloat16)
    query_grad, pair_terms = attend_back(
        bounds, begins, queries, mixed_grad, all_pairs, mixed_total, log_total
    )
    pair_grad = pair_terms.reshape(2, ctx_count, seg_len, local_width)
    for axis, bit in reversed(bits_of("ctx")):
        split = pair_grad.reshape(2, 2, -1, seg_len, local_width)
        mine = (ctx_here >> bit) & 1
        send = lax.dynamic_index_in_dim(split, 1 - mine, 1, keepdims=False)
        keep = lax.dynamic_index_in_dim(split, mine, 1, keepdims=False)
        pair_grad = keep.astype(jnp.float32) + swap(send, axis, bit).astype(jnp.float32)
        pair_grad = pair_grad.astype(jnp.bfloat16)
    key_grad, value_grad = pair_grad[0, 0], pair_grad[1, 0]
    qkv_grad_in = jnp.concatenate([query_grad, key_grad, value_grad], axis=1)
    partial_hidden = jnp.einsum(
        "te,de->td", qkv_grad_in, qkv_rows, preferred_element_type=jnp.float32
    )
    hidden_grad = pair_sum(partial_hidden)
    token_grad = middle_grad + norm_back(hidden_grad * gains[0], normed, inv_std)
    qkv_term = jnp.einsum("td,te->de", hidden, qkv_grad_in, preferred_element_type=jnp.float32)
    out_term = jnp.einsum("te,tc->ec", attn_in, mixed, preferred_element_type=jnp.float32)
    up_term = jnp.einsum("td,tf->df", hidden_two, pre_grad, preferred_element_type=jnp.float32)
    down_term = jnp.einsum("te,tf->ef", down_in, activ, preferred_element_type=jnp.float32)
    qv_term = jnp.stack(
        [
            jnp.sum(query_grad.astype(jnp.float32), axis=0),
            jnp.sum(value_grad.astype(jnp.float32), axis=0),
        ]
    )
    up_bias_term = jnp.sum(pre_grad.astype(jnp.float32), axis=0)
    out_bias_term = jnp.stack(
        [jnp.sum(attn_in.astype(jnp.float32), axis=0), jnp.sum(down_in.astype(jnp.float32), axis=0)]
    )
    gains_term = jnp.stack(
        [jnp.sum(hidden_grad * normed, axis=0), jnp.sum(hidden_two_grad * normed_two, axis=0)]
    )
    shifts_term = jnp.stack([jnp.sum(hidden_grad, axis=0), jnp.sum(hidden_two_grad, axis=0)])
    along_ctx, along_fsdp = bits_of("ctx"), bits_of("fsdp")
    ctx_first = along_ctx + along_fsdp
    fsdp_first = along_fsdp[:1] + along_ctx + along_fsdp[1:]
    parts = lax.axis_size("fsdp") * ctx_count
    down_sum = scatter_rows(down_term.astype(jnp.bfloat16), ctx_first)
    up_sum = scatter_rows(up_term.astype(jnp.bfloat16), fsdp_first)
    out_sum = scatter_rows(out_term.astype(jnp.bfloat16), ctx_first)
    qkv_sum = scatter_rows(qkv_term.astype(jnp.bfloat16), ctx_first)

    def in_parts(term):
        lead = term.shape[0]
        return term.reshape(lead, parts, -1).transpose(1, 0, 2).reshape(parts, -1)

    small = [qv_term, up_bias_term[None], out_bias_term, gains_term, shifts_term]
    small_sum = scatter_rows(
        jnp.concatenate([in_parts(term) for term in small], axis=1), ctx_first
    ).reshape(-1)
    small_sums = []
    start = 0
    for term in small:
        size = term.size // parts
        small_sums.append(small_sum[start : start + size].reshape(term.shape[0], -1))
        start += size
    return (
        output[None],
        token_grad[None],
        qkv_sum.reshape(-1, 3, local_width).transpose(1, 0, 2),
        out_sum.T,
        up_sum,
        down_sum.T,
        small_sums[0][:, None, :],
        small_sums[1],
        small_sums[2],
        small_sums[3],
        small_sums[4],
    )


def solution(mesh):
    placed = (
        P("fsdp", "ctx", None),
        P("fsdp", "ctx", None),
        P("fsdp", None),
        P(None, "fsdp", "tp"),
        P("tp", "fsdp"),
        P("fsdp", "tp"),
        P("tp", "fsdp"),
        P(None, "tp"),
        P("tp"),
        P(),
        P(),
        P(),
    )
    return jax.shard_map(
        per_device,
        mesh=mesh,
        in_specs=placed,
        out_specs=(
            P("fsdp", "ctx", None),
            P("fsdp", "ctx", None),
            P(None, ("fsdp", "ctx"), "tp"),
            P("tp", ("fsdp", "ctx")),
            P(("fsdp", "ctx"), "tp"),
            P("tp", ("fsdp", "ctx")),
            P(None, "tp", ("fsdp", "ctx")),
            P("tp", ("fsdp", "ctx")),
            P(None, ("fsdp", "ctx")),
            P(None, ("fsdp", "ctx")),
            P(None, ("fsdp", "ctx")),
        ),
        check_vma=False,
    )
```

```python
import functools

import jax
import jax.numpy as jnp
from jax import lax
from jax.experimental import pallas as pl
from jax.experimental.pallas import tpu as pltpu
from jax.sharding import PartitionSpec as P

HD = 64


EPSILON = 1e-05
NEG_LARGE = -1e30


def normalize(values):
    centre = values - jnp.mean(values, axis=-1, keepdims=True)
    variance = jnp.mean(centre * centre, axis=-1, keepdims=True)
    inv_std = lax.rsqrt(variance + EPSILON)
    return (centre * inv_std, inv_std)


def norm_back(grad_in, normed, inv_std):
    mean_grad = jnp.mean(grad_in, axis=-1, keepdims=True)
    mean_cross = jnp.mean(grad_in * normed, axis=-1, keepdims=True)
    return inv_std * (grad_in - mean_grad - normed * mean_cross)


def gelu_curve(values):
    return jax.nn.gelu(values, approximate=True)


def bits_of(axis):
    size = lax.axis_size(axis)
    return [(axis, bit) for bit in range(size.bit_length() - 1)]


def swap(values, axis, bit):
    size = lax.axis_size(axis)
    return lax.ppermute(values, axis, [(i, i ^ (1 << bit)) for i in range(size)])


def tie(*values):
    return lax.optimization_barrier(values)


def gather_rows(shard, axis, last=None):
    size = lax.axis_size(axis)
    here = lax.axis_index(axis)
    rows = shard.shape[0]
    held = shard
    offsets = [0]
    for _, bit in reversed(bits_of(axis)):
        if last is not None and bit == 0:
            held = last(held)
        held = jnp.concatenate([held, swap(held, axis, bit)], axis=0)
        offsets = offsets + [offset ^ (1 << bit) for offset in offsets]
    place = [offsets.index(offset) for offset in range(size)]
    place = jnp.array(place, jnp.int32)
    parts = [
        lax.dynamic_slice_in_dim(held, place[jnp.bitwise_xor(here, i)] * rows, rows, 0)
        for i in range(size)
    ]
    return jnp.concatenate(parts, axis=0)


def scatter_rows(terms, order, first=None):
    fsdp_bits, ctx_bits = len(bits_of("fsdp")), len(bits_of("ctx"))
    count = fsdp_bits + ctx_bits
    held = terms.reshape((2,) * count + (terms.shape[0] >> count,) + terms.shape[1:])
    for step, (axis, bit) in enumerate(order):
        dim = fsdp_bits - 1 - bit if axis == "fsdp" else count - 1 - bit
        mine = (lax.axis_index(axis) >> bit) & 1
        send = lax.dynamic_index_in_dim(held, 1 - mine, dim, keepdims=True)
        keep = lax.dynamic_index_in_dim(held, mine, dim, keepdims=True)
        received = swap(send, axis, bit)
        if first is not None and step == 0:
            received = first(received)
        held = keep.astype(jnp.float32) + received.astype(jnp.float32)
        if step < count - 1:
            held = held.astype(terms.dtype)
    return held.reshape(held.shape[count:])


def pair_sum(partial, *later):
    sent = partial.astype(jnp.bfloat16)
    total = sent.astype(jnp.float32)
    for axis, bit in bits_of("tp"):
        received = swap(total.astype(jnp.bfloat16), axis, bit)
        received, *later = tie(received, *later)
        total = total + received.astype(jnp.float32)
    return (total, *later) if later else total


BLOCK_Q = 512
BLOCK_K = 512
PAIR = 2 * HD


def half_mask(shape, dim, half):
    spots = lax.broadcasted_iota(jnp.int32, shape, dim)
    inside = (spots >= half * HD) & (spots < (half + 1) * HD)
    return jnp.where(inside, 1.0, 0.0).astype(jnp.bfloat16)


def allowed_pairs(shape, key_start, query_start, begin):
    key_pos = key_start + lax.broadcasted_iota(jnp.int32, shape, 0)
    query_pos = query_start + lax.broadcasted_iota(jnp.int32, shape, 1)
    return (key_pos <= query_pos) & (key_pos >= begin)


def mix_kernel(bounds, q_ref, k_ref, v_ref, begin_ref, mix_ref, total_ref, lse_ref, vt_ref):
    step = pl.program_id(1)
    width = q_ref.shape[0]
    block = min(BLOCK_K, k_ref.shape[0])

    @pl.when(step == 0)
    def _():
        vt_ref[...] = v_ref[...].T

    query_t = (q_ref[...] * jnp.bfloat16(0.125)).T
    query_parts = [query_t * half_mask(query_t.shape, 0, half) for half in range(2)]
    begin = begin_ref[...]
    query_start = bounds[4, step]

    def body(masked, block_id, carry):
        start = pl.multiple_of(block_id * block, block)
        keys = k_ref[pl.ds(start, block), :]
        if masked:
            allowed = allowed_pairs((block, width), start, query_start, begin)
        out = []
        for half in range(2):
            run_max, run_sum, total = carry[half]
            scores = jnp.dot(keys, query_parts[half], preferred_element_type=jnp.float32)
            if masked:
                scores = jnp.where(allowed, scores, NEG_LARGE)
            new_max = jnp.maximum(run_max, jnp.max(scores, axis=0, keepdims=True))
            weights = jnp.exp(scores - new_max)
            decay = jnp.exp(run_max - new_max)
            values_t = vt_ref[half * HD : (half + 1) * HD, pl.ds(start, block)]
            out.append(
                (
                    new_max,
                    run_sum * decay + jnp.sum(weights, axis=0, keepdims=True),
                    total * decay
                    + jnp.dot(
                        values_t, weights.astype(jnp.bfloat16), preferred_element_type=jnp.float32
                    ),
                )
            )
        return tuple(out)

    empty = (
        jnp.full((1, width), NEG_LARGE, jnp.float32),
        jnp.zeros((1, width), jnp.float32),
        jnp.zeros((HD, width), jnp.float32),
    )
    carry = (empty, empty)
    for part, masked in enumerate((True, False, True)):
        carry = lax.fori_loop(
            bounds[part, step], bounds[part + 1, step], functools.partial(body, masked), carry
        )
    for half in range(2):
        run_max, run_sum, total = carry[half]
        total_ref[half * HD : (half + 1) * HD, :] = total / run_sum
        lse_ref[0, half : half + 1, :] = run_max + jnp.log(run_sum)
    mix_ref[...] = total_ref[...].T.astype(jnp.bfloat16)


def grad_kernel(
    bounds, q_ref, g_ref, k_ref, v_ref, begin_ref, total_ref, lse_ref,
    dq_ref, dkv_ref, kt_ref, dk_ref, dv_ref,
):
    step = pl.program_id(1)
    width = q_ref.shape[0]
    block = min(BLOCK_K, k_ref.shape[0])

    @pl.when(step == 0)
    def _():
        kt_ref[...] = k_ref[...].T
        dk_ref[...] = jnp.zeros_like(dk_ref)
        dv_ref[...] = jnp.zeros_like(dv_ref)

    query = q_ref[...] * jnp.bfloat16(0.125)
    grad = g_ref[...]
    query_t = query.T
    grad_t = grad.T
    product = grad_t.astype(jnp.float32) * total_ref[...]
    parts = []
    for half in range(2):
        down = half_mask(query_t.shape, 0, half)
        along = half_mask(query.shape, 1, half)
        parts.append(
            (
                query * along,
                query_t * down,
                grad * along,
                grad_t * down,
                jnp.sum(product[half * HD : (half + 1) * HD, :], axis=0, keepdims=True),
                lse_ref[0, half : half + 1, :],
            )
        )
    begin = begin_ref[...]
    query_start = bounds[4, step]

    def body(masked, block_id, carry):
        start = pl.multiple_of(block_id * block, block)
        spots = pl.ds(start, block)
        keys = k_ref[spots, :]
        values = v_ref[spots, :]
        if masked:
            allowed = allowed_pairs((block, width), start, query_start, begin)
        out = []
        key_sum = dk_ref[spots, :]
        value_sum = dv_ref[spots, :]
        for half in range(2):
            query_n, query_t, grad_n, grad_t, delta, lse = parts[half]
            scores = jnp.dot(keys, query_t, preferred_element_type=jnp.float32)
            if masked:
                scores = jnp.where(allowed, scores, NEG_LARGE)
            weights = jnp.exp(scores - lse)
            weight_grad = jnp.dot(values, grad_t, preferred_element_type=jnp.float32)
            score_grad = (weights * (weight_grad - delta)).astype(jnp.bfloat16)
            value_sum = value_sum + jnp.dot(
                weights.astype(jnp.bfloat16), grad_n, preferred_element_type=jnp.float32
            )
            key_sum = key_sum + jnp.dot(score_grad, query_n, preferred_element_type=jnp.float32)
            keys_t = kt_ref[half * HD : (half + 1) * HD, spots]
            out.append(
                carry[half] + jnp.dot(keys_t, score_grad, preferred_element_type=jnp.float32)
            )
        dk_ref[spots, :] = key_sum
        dv_ref[spots, :] = value_sum
        return tuple(out)

    carry = (jnp.zeros((HD, width), jnp.float32),) * 2
    for part, masked in enumerate((True, False, True)):
        carry = lax.fori_loop(
            bounds[part, step], bounds[part + 1, step], functools.partial(body, masked), carry
        )
    dq_ref[...] = (jnp.concatenate(carry, axis=0) * 0.125).T.astype(jnp.bfloat16)

    @pl.when(step == pl.num_programs(1) - 1)
    def _():
        dkv_ref[0] = dk_ref[...].astype(jnp.bfloat16)
        dkv_ref[1] = dv_ref[...].astype(jnp.bfloat16)


def attention_bounds(first_pos, seg_len, row_len, begins):
    width, block = min(BLOCK_Q, seg_len), min(BLOCK_K, row_len)
    count = seg_len // width
    starts = first_pos + jnp.arange(count, dtype=jnp.int32) * width
    low = begins[::width] // block
    end = (starts + width - 1) // block + 1
    inner = jnp.clip((begins[width - 1 :: width] + block - 1) // block, low, end)
    outer = jnp.clip((starts + 1) // block, inner, end)
    return jnp.stack([low, inner, outer, end, starts]).astype(jnp.int32)


def attend(bounds, begins, queries, pairs):
    seg_len, local_width = queries.shape
    row_len = pairs.shape[0]
    count = local_width // PAIR
    width = min(BLOCK_Q, seg_len)
    work = count * 2 * seg_len * row_len
    return pl.pallas_call(
        mix_kernel,
        grid_spec=pltpu.PrefetchScalarGridSpec(
            num_scalar_prefetch=1,
            grid=(count, seg_len // width),
            in_specs=[
                pl.BlockSpec((width, PAIR), lambda p, i, b: (i, p)),
                pl.BlockSpec((row_len, PAIR), lambda p, i, b: (0, p)),
                pl.BlockSpec((row_len, PAIR), lambda p, i, b: (0, p + count)),
                pl.BlockSpec((1, width), lambda p, i, b: (0, i)),
            ],
            out_specs=[
                pl.BlockSpec((width, PAIR), lambda p, i, b: (i, p)),
                pl.BlockSpec((PAIR, width), lambda p, i, b: (p, i)),
                pl.BlockSpec((1, 2, width), lambda p, i, b: (p, 0, i)),
            ],
            scratch_shapes=[pltpu.VMEM((PAIR, row_len), jnp.bfloat16)],
        ),
        out_shape=[
            jax.ShapeDtypeStruct((seg_len, local_width), jnp.bfloat16),
            jax.ShapeDtypeStruct((local_width, seg_len), jnp.float32),
            jax.ShapeDtypeStruct((count, 2, seg_len), jnp.float32),
        ],
        compiler_params=pltpu.CompilerParams(vmem_limit_bytes=48 * 1024 * 1024),
        cost_estimate=pl.CostEstimate(
            flops=work * 4 * PAIR, bytes_accessed=6 * 2**20, transcendentals=work
        ),
        name="attn_mix",
    )(bounds, queries, pairs, pairs, begins[None])


def attend_back(bounds, begins, queries, grads, pairs, totals, lse, first, number):
    seg_len, local_width = queries.shape
    row_len = pairs.shape[0]
    count = local_width // PAIR
    width = min(BLOCK_Q, seg_len)
    work = number * 2 * seg_len * row_len
    return pl.pallas_call(
        grad_kernel,
        grid_spec=pltpu.PrefetchScalarGridSpec(
            num_scalar_prefetch=1,
            grid=(number, seg_len // width),
            in_specs=[
                pl.BlockSpec((width, PAIR), lambda p, i, b: (i, p + first)),
                pl.BlockSpec((width, PAIR), lambda p, i, b: (i, p + first)),
                pl.BlockSpec((row_len, PAIR), lambda p, i, b: (0, p + first)),
                pl.BlockSpec((row_len, PAIR), lambda p, i, b: (0, p + first + count)),
                pl.BlockSpec((1, width), lambda p, i, b: (0, i)),
                pl.BlockSpec((PAIR, width), lambda p, i, b: (p + first, i)),
                pl.BlockSpec((1, 2, width), lambda p, i, b: (p + first, 0, i)),
            ],
            out_specs=[
                pl.BlockSpec((width, PAIR), lambda p, i, b: (i, p)),
                pl.BlockSpec((2, row_len, PAIR), lambda p, i, b: (0, 0, p)),
            ],
            scratch_shapes=[
                pltpu.VMEM((PAIR, row_len), jnp.bfloat16),
                pltpu.VMEM((row_len, PAIR), jnp.float32),
                pltpu.VMEM((row_len, PAIR), jnp.float32),
            ],
        ),
        out_shape=[
            jax.ShapeDtypeStruct((seg_len, number * PAIR), jnp.bfloat16),
            jax.ShapeDtypeStruct((2, row_len, number * PAIR), jnp.bfloat16),
        ],
        compiler_params=pltpu.CompilerParams(vmem_limit_bytes=48 * 1024 * 1024),
        cost_estimate=pl.CostEstimate(
            flops=work * 8 * PAIR, bytes_accessed=12 * 2**20, transcendentals=work
        ),
        name="attn_grad",
    )(bounds, queries, grads, pairs, pairs, begins[None], totals, lse)


def per_device(
    tokens,
    cotangent,
    lengths,
    w_qkv,
    w_out,
    w_up,
    w_down,
    qv_bias,
    up_bias,
    out_bias,
    gains,
    shifts,
):
    stream = tokens[0].astype(jnp.float32)
    grad_out = cotangent[0]
    seg_len = stream.shape[0]
    ctx_count = lax.axis_size("ctx")
    ctx_here = lax.axis_index("ctx")
    row_len = seg_len * ctx_count
    first_pos = ctx_here * seg_len
    seq_lens = lengths[0]
    seq_starts = jnp.cumsum(seq_lens, dtype=jnp.int32) - seq_lens

    query_pos = first_pos + jnp.arange(seg_len, dtype=jnp.int32)
    begins = jnp.max(
        jnp.where(query_pos[:, None] >= seq_starts[None, :], seq_starts[None, :], 0), axis=1
    ).astype(jnp.int32)
    local_width = w_qkv.shape[2]
    bounds = attention_bounds(first_pos, seg_len, row_len, begins)
    waiting = [w_up, w_out, w_down]

    def release(held):
        held, *waiting[:] = tie(held, *waiting)
        return held

    qkv_rows = gather_rows(
        jnp.concatenate([w_qkv[0], w_qkv[1], w_qkv[2]], axis=1), "fsdp", release
    )
    w_up, w_out, w_down = waiting
    both_rows = gather_rows(jnp.concatenate([w_up, w_out.T], axis=1), "fsdp")
    up_full, out_rows = both_rows[:, : w_up.shape[1]], both_rows[:, w_up.shape[1] :]
    normed, inv_std = normalize(stream)
    hidden = (normed * gains[0] + shifts[0]).astype(jnp.bfloat16)
    projected = jnp.dot(hidden, qkv_rows, preferred_element_type=jnp.float32)
    queries = (projected[:, :local_width] + qv_bias[0]).astype(jnp.bfloat16)
    pair_bias = jnp.concatenate([jnp.zeros_like(qv_bias[1]), qv_bias[1]])
    pairs = (projected[:, local_width:] + pair_bias).astype(jnp.bfloat16)
    all_pairs = gather_rows(pairs, "ctx")
    mixed, mixed_total, log_total = attend(bounds, begins, queries, all_pairs)
    waiting = [mixed]
    down_rows = gather_rows(w_down.T, "fsdp", release)
    mixed = waiting[0]
    partial_attn = jnp.einsum("tc,ec->te", mixed, out_rows, preferred_element_type=jnp.float32)
    middle = (
        stream + pair_sum(partial_attn) + out_bias[0]
    )
    normed_two, inv_two = normalize(middle)
    hidden_two = (normed_two * gains[1] + shifts[1]).astype(jnp.bfloat16)
    pre_act = jnp.dot(hidden_two, up_full, preferred_element_type=jnp.float32) + up_bias
    activ_exact, gelu_pull = jax.vjp(gelu_curve, pre_act)
    activ = activ_exact.astype(jnp.bfloat16)
    partial_ff = jnp.einsum("tf,ef->te", activ, down_rows, preferred_element_type=jnp.float32)
    output = (
        middle + pair_sum(partial_ff) + out_bias[1]
    )
    down_in = grad_out.astype(jnp.bfloat16)
    act_grad = jnp.einsum("te,ef->tf", down_in, down_rows, preferred_element_type=jnp.float32)
    pre_grad = gelu_pull(act_grad)[0].astype(jnp.bfloat16)
    partial_two = jnp.einsum("tf,df->td", pre_grad, up_full, preferred_element_type=jnp.float32)
    up_term = jnp.einsum("td,tf->df", hidden_two, pre_grad, preferred_element_type=jnp.float32)
    down_term = jnp.einsum("te,tf->ef", down_in, activ, preferred_element_type=jnp.float32)
    hidden_two_grad = pair_sum(partial_two)
    middle_grad = grad_out + norm_back(hidden_two_grad * gains[1], normed_two, inv_two)
    attn_in = middle_grad.astype(jnp.bfloat16)
    mixed_grad = jnp.einsum(
        "te,ec->tc", attn_in, out_rows, preferred_element_type=jnp.float32
    ).astype(jnp.bfloat16)
    along_ctx, along_fsdp = bits_of("ctx"), bits_of("fsdp")
    ctx_first = along_ctx + along_fsdp
    fsdp_first = along_fsdp[:1] + along_ctx + along_fsdp[1:]
    heads_pairs = local_width // PAIR
    early = (heads_pairs + 2) // 3
    query_grads, pair_grads = [], []
    waiting = [mixed_grad]
    for first, number in ((0, early), (early, heads_pairs - early)):
        query_part, pair_terms = attend_back(
            bounds, begins, queries, waiting[0], all_pairs, mixed_total, log_total, first, number
        )
        if first == 0:
            waiting = [mixed_grad, query_part]
            down_sum = scatter_rows(down_term.astype(jnp.bfloat16), ctx_first, release)
            up_sum = scatter_rows(up_term.astype(jnp.bfloat16), fsdp_first, release)
            query_part = waiting[1]
        pair_grad = pair_terms.reshape(2, ctx_count, seg_len, number * PAIR)
        for axis, bit in reversed(bits_of("ctx")):
            split = pair_grad.reshape(2, 2, -1, seg_len, number * PAIR)
            mine = (ctx_here >> bit) & 1
            send = lax.dynamic_index_in_dim(split, 1 - mine, 1, keepdims=False)
            keep = lax.dynamic_index_in_dim(split, mine, 1, keepdims=False)
            pair_grad = keep.astype(jnp.float32) + swap(send, axis, bit).astype(jnp.float32)
            pair_grad = pair_grad.astype(jnp.bfloat16)
        query_grads.append(query_part)
        pair_grads.append(pair_grad[:, 0])
    query_grad = jnp.concatenate(query_grads, axis=1)
    key_grad = jnp.concatenate([part[0] for part in pair_grads], axis=1)
    value_grad = jnp.concatenate([part[1] for part in pair_grads], axis=1)
    qkv_grad_in = jnp.concatenate([query_grad, key_grad, value_grad], axis=1)
    partial_hidden = jnp.einsum(
        "te,de->td", qkv_grad_in, qkv_rows, preferred_element_type=jnp.float32
    )
    query_term = jnp.einsum("td,te->de", hidden, query_grad, preferred_element_type=jnp.float32)
    pair_term = jnp.einsum(
        "td,te->de", hidden, qkv_grad_in[:, local_width:], preferred_element_type=jnp.float32
    )
    hidden_grad, pair_term = pair_sum(partial_hidden, pair_term.astype(jnp.bfloat16))
    token_grad = middle_grad + norm_back(hidden_grad * gains[0], normed, inv_std)
    out_term = jnp.einsum("te,tc->ec", attn_in, mixed, preferred_element_type=jnp.float32)
    qv_term = jnp.stack(
        [
            jnp.sum(query_grad.astype(jnp.float32), axis=0),
            jnp.sum(value_grad.astype(jnp.float32), axis=0),
        ]
    )
    up_bias_term = jnp.sum(pre_grad.astype(jnp.float32), axis=0)
    out_bias_term = jnp.stack(
        [jnp.sum(attn_in.astype(jnp.float32), axis=0), jnp.sum(down_in.astype(jnp.float32), axis=0)]
    )
    gains_term = jnp.stack(
        [jnp.sum(hidden_grad * normed, axis=0), jnp.sum(hidden_two_grad * normed_two, axis=0)]
    )
    shifts_term = jnp.stack([jnp.sum(hidden_grad, axis=0), jnp.sum(hidden_two_grad, axis=0)])
    parts = lax.axis_size("fsdp") * ctx_count
    out_sum = scatter_rows(out_term.astype(jnp.bfloat16), ctx_first)
    query_sum = scatter_rows(query_term.astype(jnp.bfloat16), fsdp_first)
    pair_sums = scatter_rows(pair_term, ctx_first)

    def in_parts(term):
        lead = term.shape[0]
        return term.reshape(lead, parts, -1).transpose(1, 0, 2).reshape(parts, -1)

    small = [qv_term, up_bias_term[None], out_bias_term, gains_term, shifts_term]
    small_terms, token_grad = tie(
        jnp.concatenate([in_parts(term) for term in small], axis=1), token_grad
    )
    small_sum = scatter_rows(small_terms, ctx_first).reshape(-1)
    small_sums = []
    start = 0
    for term in small:
        size = term.size // parts
        small_sums.append(small_sum[start : start + size].reshape(term.shape[0], -1))
        start += size
    return (
        output[None],
        token_grad[None],
        jnp.stack([query_sum, pair_sums[:, :local_width], pair_sums[:, local_width:]]),
        out_sum.T,
        up_sum,
        down_sum.T,
        small_sums[0][:, None, :],
        small_sums[1],
        small_sums[2],
        small_sums[3],
        small_sums[4],
    )


def solution(mesh):
    placed = (
        P("fsdp", "ctx", None),
        P("fsdp", "ctx", None),
        P("fsdp", None),
        P(None, "fsdp", "tp"),
        P("tp", "fsdp"),
        P("fsdp", "tp"),
        P("tp", "fsdp"),
        P(None, "tp"),
        P("tp"),
        P(),
        P(),
        P(),
    )
    return jax.shard_map(
        per_device,
        mesh=mesh,
        in_specs=placed,
        out_specs=(
            P("fsdp", "ctx", None),
            P("fsdp", "ctx", None),
            P(None, ("fsdp", "ctx"), "tp"),
            P("tp", ("fsdp", "ctx")),
            P(("fsdp", "ctx"), "tp"),
            P("tp", ("fsdp", "ctx")),
            P(None, "tp", ("fsdp", "ctx")),
            P("tp", ("fsdp", "ctx")),
            P(None, ("fsdp", "ctx")),
            P(None, ("fsdp", "ctx")),
            P(None, ("fsdp", "ctx")),
        ),
        check_vma=False,
    )
```
